32 devices in a mesh: section: 2 (over x), tensor: 4 (over y, core), dp: 4 (over z).
Axes of the slice: x: 2, y: 2, z: 4, core: 2. Of those that a mesh axis runs over, the one named last changes fastest.
Arguments:
- tokens: bfloat16 [8, 1024, 768], P('dp', 'tensor'), may hold values from -6 to 6
- w_qkv: bfloat16 [2, 768, 3, 768], P('section', None, None, 'tensor'), may hold values from -0.109375 to 0.109375
- w_out: bfloat16 [2, 768, 768], P('section', 'tensor'), may hold values from -1.75 to 1.75
- w_up: bfloat16 [2, 768, 3072], P('section', None, 'tensor'), may hold values from -0.21875 to 0.21875
- w_down: bfloat16 [2, 3072, 768], P('section', 'tensor'), may hold values from -0.109375 to 0.109375
- norm_params: float32 [2, 4, 768], P('section'), may hold values from -1 to 1.5, as said below
- features: bfloat16 [2, 64, 256], P('section'), may hold values from -5 to 5
- block_lists: int32 [8, 12, 16, 4], P('dp', 'tensor'), may hold values from 0 to 15, as said below
- long_flags: int32 [8], P('dp'), may hold values from 0 to 1, as said below
- out_grad: bfloat16 [8, 1024, 768], P('dp', 'tensor'), may hold values from -6 to 6
Outputs:
- acts: bfloat16 [2, 8, 1024, 768], P('section', 'dp', 'tensor')
- input_grads: float32 [2, 8, 1024, 768], P('section', 'dp', 'tensor')
- g_qkv: float32 [2, 768, 3, 768], P('section', None, None, 'tensor')
- g_out: float32 [2, 768, 768], P('section', 'tensor')
- g_up: float32 [2, 768, 3072], P('section', None, 'tensor')
- g_down: float32 [2, 3072, 768], P('section', 'tensor')
- g_norm: float32 [2, 4, 768], P('section')
The draws below stay inside these ranges and needn't reach their ends.
Inputs may be any that keep to these rules, and one draw needn't show every extreme that they name: `long_flags`: every data group has at least one micro-batch of each kind. `block_lists`: each list names 4 distinct blocks of the same micro-batch; blocks in the other sequence of a two-sequence micro-batch are left out by the mask. `norm_params`: rows 0 and 2 are gains, rows 1 and 3 biases.
All inputs are finite; a program needn't handle non-finite values.
Results may differ from the reference program's by a relative error of at most 0.02.
Values may be sent and summed in bfloat16 or wider, within the bound.
No kernel may reach another device: no remote copies, remote signals or barrier semaphores. Data moves between devices by JAX's collectives and lax.ppermute only.
A program may use at most 384 MiB of HBM per device.

```python
import jax
import jax.numpy as jnp
from jax import lax

D = 768
H = 12
FF = 3072
HD = 64
M = 256
BLK = 64
K = 4
MBTOK = 1024
MICRO = 2
N_DP = 4


def draw_norm_params(key, part):
    key = jax.random.fold_in(key, 13)
    key_gain, key_bias = jax.random.split(key)
    gains = jnp.clip(1.0 + 0.1 * jax.random.normal(key_gain, (2, 2, D), jnp.float32), 0.5, 1.5)
    biases = jnp.clip(0.3 * jax.random.normal(key_bias, (2, 2, D), jnp.float32), -1.0, 1.0)
    return jnp.stack([gains[:, 0], biases[:, 0], gains[:, 1], biases[:, 1]], axis=1)


def draw_block_lists(key, part):
    key = jax.random.fold_in(key, 12)
    blocks = MBTOK // BLK
    ranks = jax.random.randint(key, (N_DP * MICRO, H, blocks, blocks), 0, 1 << 20, jnp.int32)
    ranks = ranks * blocks + jnp.arange(blocks, dtype=jnp.int32)
    chosen = lax.top_k(ranks, K)[1]
    return chosen.astype(jnp.int32)


def draw_long_flags(key, part):
    key = jax.random.fold_in(key, 11)
    key_base, key_place = jax.random.split(key)
    base = jax.random.randint(key_base, (N_DP, MICRO), 0, 2, jnp.int32)
    place = jax.random.randint(key_place, (N_DP, 1), 0, MICRO, jnp.int32)
    column = jnp.arange(MICRO, dtype=jnp.int32)[None, :]
    flags = jnp.where(column == place, 1, jnp.where(column == (place + 1) % MICRO, 0, base))
    return flags.reshape(N_DP * MICRO).astype(jnp.int32)


def block_levels(key, extent, shards, smallest, high):
    def one(axis_at, shards_of):
        heights = jax.random.uniform(jax.random.fold_in(jax.random.fold_in(key, 6), axis_at), (shards_of,), jnp.float32, smallest / len(shards), high / len(shards))
        return jnp.repeat(jnp.exp(heights), extent[axis_at] // shards_of).reshape((-1,) + (1,) * (len(extent) - axis_at - 1))

    factor_of = one(*shards[0])
    for cut in shards[1:]:
        factor_of = factor_of * one(*cut)
    return factor_of


def normal_values(own_key, extent, scale, limit, pieces=(), kind=jnp.bfloat16):
    entries = jax.random.normal(own_key, extent, jnp.float32) * scale
    if len(pieces) > 0:
        entries = block_levels(own_key, extent, pieces, -0.22, 0.18) * entries
    return jnp.clip(entries, min=-limit, max=limit).astype(kind)


def setup_inputs(seed: int = 0) -> dict:
    arg_keys = jax.random.split(jax.random.key(seed), 11)
    return {
        "tokens": normal_values(arg_keys[0], (N_DP * MICRO, MBTOK, D), 1.0, 6.0, ((0, 4), (1, 4))),
        "w_qkv": normal_values(arg_keys[1], (2, D, 3, D), (4 * D) ** -0.5, 0.109375, ((0, 2), (3, 4))),
        "w_out": normal_values(arg_keys[2], (2, D, D), (D // 64) ** -0.5, 1.75, ((0, 2), (1, 4))),
        "w_up": normal_values(arg_keys[3], (2, D, FF), D ** -0.5, 0.21875, ((0, 2), (2, 4))),
        "w_down": normal_values(arg_keys[4], (2, FF, D), FF ** -0.5, 0.109375, ((0, 2), (1, 4))),
        "norm_params": draw_norm_params(jax.random.fold_in(arg_keys[10], 71), 0),
        "features": normal_values(arg_keys[6], (2, HD, M), 1.0, 5.0, ((0, 2),)),
        "block_lists": draw_block_lists(jax.random.fold_in(arg_keys[10], 71), 0),
        "long_flags": draw_long_flags(jax.random.fold_in(arg_keys[10], 71), 0),
        "out_grad": normal_values(arg_keys[9], (N_DP * MICRO, MBTOK, D), 1.0, 6.0, ((0, 4), (1, 4))),
    }


norm_eps = 1e-05

@jax.custom_vjp
def low(v):
    return lax.optimization_barrier(v.astype(jnp.bfloat16)).astype(jnp.float32)

@jax.custom_vjp
def low_back(v):
    return v

def low_keep(v):
    return (low(v), None)

def low_pass(kept, grad):
    return (grad,)

def back_keep(v):
    return (v, None)

def back_low(kept, grad):
    return (low(grad),)
low.defvjp(low_keep, low_pass)
low_back.defvjp(back_keep, back_low)

def layer_norm(rows_in, gain, bias):
    center = rows_in - lax.optimization_barrier(jnp.mean(rows_in, axis=-1, keepdims=True))
    spread = lax.optimization_barrier(jnp.mean(center * center, axis=-1, keepdims=True))
    return center * lax.rsqrt(spread + norm_eps) * gain + bias

def attend(query, key_rows, value_rows, feature_map, block_ids, long_flag):
    head_count, length, head_dim = query.shape
    blocks = length // BLK
    half_length = length // 2
    highest_precision = lax.Precision.HIGHEST
    feat_count = feature_map.shape[1]

    def featurize(rows_in):
        proj = jnp.einsum('htd,dm->htm', rows_in, feature_map, precision=highest_precision) * head_dim ** (-0.25)
        sq_norm = lax.optimization_barrier(jnp.sum(rows_in * rows_in, axis=-1, keepdims=True)) * (0.5 * head_dim ** (-0.5))
        return jnp.exp(proj - sq_norm) * feat_count ** (-0.5)
    query_features = featurize(query)
    key_features = featurize(key_rows)
    long_mask = long_flag.astype(jnp.float32)
    saved_values_low = jnp.einsum('gsi,gsx->gix', key_features[:, :half_length], value_rows[:, :half_length], precision=highest_precision)
    saved_values_high = jnp.einsum('gsi,gsx->gix', key_features[:, half_length:], value_rows[:, half_length:], precision=highest_precision)
    ones_low = lax.optimization_barrier(jnp.sum(key_features[:, :half_length], axis=1))
    ones_high = lax.optimization_barrier(jnp.sum(key_features[:, half_length:], axis=1))
    first_saved_values = saved_values_low + long_mask * saved_values_high
    second_saved_values = saved_values_high + long_mask * saved_values_low
    first_one = ones_low + long_mask * ones_high
    second_one = ones_high + long_mask * ones_low
    performer_numerator = jnp.concatenate([jnp.einsum('cou,cuw->cow', query_features[:, :half_length], first_saved_values, precision=highest_precision), jnp.einsum('cou,cuw->cow', query_features[:, half_length:], second_saved_values, precision=highest_precision)], axis=1)
    denom_perf = jnp.concatenate([jnp.einsum('htm,hm->ht', query_features[:, :half_length], first_one, precision=highest_precision), jnp.einsum('htm,hm->ht', query_features[:, half_length:], second_one, precision=highest_precision)], axis=1)
    one_hot = (block_ids[..., None] == jnp.arange(blocks, dtype=jnp.int32)).astype(jnp.float32)
    listed = block_ids.shape[-1]

    def select(table):
        table_blocks = table.reshape(head_count, blocks, BLK, table.shape[-1])
        chosen = jnp.einsum('hbkc,hcrd->hbkrd', one_hot, table_blocks, precision=highest_precision)
        return chosen.reshape(head_count, blocks, listed * BLK, table.shape[-1])
    key_sel = select(key_rows)
    value_sel = select(value_rows)
    feat_sel = select(key_features)
    query_blocks = query.reshape(head_count, blocks, BLK, head_dim)
    qfeat_blocks = query_features.reshape(head_count, blocks, BLK, feat_count)
    scores = jnp.einsum('hbqd,hbjd->hbqj', query_blocks, key_sel, precision=highest_precision) * head_dim ** (-0.5)
    estimate = jnp.einsum('hbqm,hbjm->hbqj', qfeat_blocks, feat_sel, precision=highest_precision)
    upper_half = (jnp.arange(blocks, dtype=jnp.int32) >= blocks // 2).astype(jnp.int32)
    query_seg = jnp.where(long_flag == 1, 0, upper_half)
    key_seg = jnp.where(long_flag == 1, 0, (block_ids >= blocks // 2).astype(jnp.int32))
    usable = (key_seg == query_seg[None, :, None]).astype(jnp.float32)
    usable = jnp.repeat(usable, BLK, axis=-1)[:, :, None, :]
    correction = (jnp.exp(scores) - estimate) * usable
    numer_sparse = jnp.einsum('hbqj,hbjd->hbqd', low(correction), value_sel, precision=highest_precision)
    denom_sparse = lax.optimization_barrier(jnp.sum(correction, axis=-1))
    numerator = performer_numerator + numer_sparse.reshape(head_count, length, head_dim)
    denominator = denom_perf + denom_sparse.reshape(head_count, length)
    return numerator / denominator[..., None]

def one_layer(rows_in, w_q, w_o, w_u, w_d, norms, feature_map, block_ids, long_flag):
    highest_precision = lax.Precision.HIGHEST
    length = rows_in.shape[0]
    normed = low(layer_norm(rows_in, norms[0], norms[1]))
    packed = low(low_back(jnp.dot(normed, w_q.reshape(D, 3 * D), precision=highest_precision)))
    shaped = packed.reshape(length, 3, H, HD).transpose(1, 2, 0, 3)
    heads_out = attend(shaped[0], shaped[1], shaped[2], feature_map, block_ids, long_flag)
    attn = low(low_back(heads_out.transpose(1, 0, 2).reshape(length, D)))
    middle = rows_in + low_back(jnp.dot(attn, w_o, precision=highest_precision))
    mixed = low(layer_norm(middle, norms[2], norms[3]))
    hidden = low_back(jnp.dot(mixed, w_u, precision=highest_precision))
    activ = low(jax.nn.gelu(hidden, approximate=False))
    return middle + jnp.dot(activ, w_d, precision=highest_precision)

def reference(tokens, w_qkv, w_out, w_up, w_down, norm_params, features, block_lists, long_flags, out_grad):
    start_rows = tokens.astype(jnp.float32)
    feature_maps = features.astype(jnp.float32)

    def run_layer(layer_no, inputs, w_q, w_o, w_u, w_d, norms):

        def single(item):
            rows_in, block_ids, long_flag = item
            return one_layer(rows_in, w_q[layer_no], w_o[layer_no], w_u[layer_no], w_d[layer_no], norms[layer_no], feature_maps[layer_no], block_ids, long_flag)
        return lax.map(jax.checkpoint(single), (inputs, block_lists, long_flags))

    def forward(inputs, probe, w_q, w_o, w_u, w_d, norms):
        first_out = run_layer(0, inputs, w_q, w_o, w_u, w_d, norms)
        passed = low(low_back(first_out)) + probe
        return (run_layer(1, passed, w_q, w_o, w_u, w_d, norms), first_out)
    probe = jnp.zeros_like(start_rows)
    outputs, pull_back = jax.vjp(forward, start_rows, probe, w_qkv.astype(jnp.float32), w_out.astype(jnp.float32), w_up.astype(jnp.float32), w_down.astype(jnp.float32), norm_params)
    last_out, first_out = outputs
    grads = pull_back((out_grad.astype(jnp.float32), jnp.zeros_like(first_out)))
    start_grad, probe_grad, grad_q, grad_o, grad_u, grad_d, grad_n = grads
    acts = jnp.stack([first_out, last_out]).astype(jnp.bfloat16)
    input_grads = jnp.stack([start_grad, probe_grad])
    return (acts, input_grads, grad_q, grad_o, grad_u, grad_d, grad_n)
```

```python
import functools
import math

import jax
import jax.numpy as jnp
from jax import lax
from jax.experimental import pallas as pl
from jax.experimental.pallas import tpu as pltpu
from jax.sharding import PartitionSpec as P

HD = 64
BLK = 64
LANES = 128
EPS = 1e-05
LOG2E = math.log2(math.e)
F32 = jnp.float32
BF = jnp.bfloat16
MIB = 1 << 20


def nn(a, b):
    return lax.dot_general(a, b, (((1,), (0,)), ((), ())), preferred_element_type=F32)


def nt(a, b):
    return lax.dot_general(a, b, (((1,), (1,)), ((), ())), preferred_element_type=F32)


def tn(a, b):
    return lax.dot_general(a, b, (((0,), (0,)), ((), ())), preferred_element_type=F32)


def lanes_of(shape):
    return lax.broadcasted_iota(jnp.int32, shape, len(shape) - 1)


def flip(x):
    return pltpu.roll(x, HD, 1)


def vmem_spec():
    return pl.BlockSpec(memory_space=pltpu.VMEM)


def smem_spec():
    return pl.BlockSpec(memory_space=pltpu.SMEM)


def bytes_of(x):
    return math.prod(x.shape) * x.dtype.itemsize


def ignoring(body, count):
    def inner(*refs):
        return body(*refs[count:])

    return inner


def any_spec():
    return pl.BlockSpec(memory_space=pl.ANY)


def run_kernel(body, name, outs, scalars, arrays, scratch=(), us=1.0, extra=3 * MIB, deps=()):
    outs = [jax.ShapeDtypeStruct(s, d) for s, d in outs]
    total = sum(bytes_of(a) for a in arrays) + sum(bytes_of(o) for o in outs)
    held = sum(math.prod(s) * jnp.dtype(d).itemsize for s, d in scratch)
    return pl.pallas_call(
        ignoring(body, len(deps)),
        name=name,
        out_shape=outs,
        in_specs=[any_spec()] * len(deps)
        + [smem_spec()] * len(scalars)
        + [vmem_spec()] * len(arrays),
        out_specs=[vmem_spec()] * len(outs),
        scratch_shapes=[pltpu.VMEM(s, d) for s, d in scratch],
        compiler_params=pltpu.CompilerParams(vmem_limit_bytes=held + extra),
        cost_estimate=cost(us, total),
    )(*deps, *scalars, *arrays)


def cost(us, total):
    return pl.CostEstimate(flops=int(us * 1e5), bytes_accessed=total // 1000, transcendentals=0)


def run_heads(
    body, name, heads, outs, scalars, shared, per_head, scratch=(), us=1.0, extra=2 * MIB, deps=(), into=()
):
    first, end, total = heads
    count = end - first
    kinds = [
        jax.ShapeDtypeStruct(
            o[0] if o[2] == "whole" else ((total if o[2] == "hbm" else count),) + o[0], o[1]
        )
        for o in outs
    ]
    part = sum(bytes_of(a) // a.shape[0] for a in per_head)
    part += sum(bytes_of(k) // (1 if o[2] == "whole" else k.shape[0]) for k, o in zip(kinds, outs))
    held = (2 if count > 1 else 1) * part
    held += sum(math.prod(s) * jnp.dtype(d).itemsize for s, d in scratch)

    def whole(x):
        return pl.BlockSpec(x.shape, lambda h: (0,) * len(x.shape))

    def one(x, start):
        rest = (0,) * (len(x.shape) - 1)
        return pl.BlockSpec((1,) + x.shape[1:], lambda h: (h + start,) + rest)

    out_specs = []
    for k, o in zip(kinds, outs):
        if o[2] == "whole":
            out_specs.append(whole(k))
        else:
            out_specs.append(one(k, first if o[2] == "hbm" else 0))
    skipped = (*into, *deps)
    return pl.pallas_call(
        ignoring(body, len(skipped)),
        name=name,
        grid=(count,),
        out_shape=[
            pltpu.HBM(k.shape, k.dtype) if o[2] == "hbm" else k for k, o in zip(kinds, outs)
        ],
        in_specs=[any_spec()] * len(skipped)
        + [smem_spec()] * len(scalars)
        + [vmem_spec()] * len(shared)
        + [one(x, first) for x in per_head],
        out_specs=out_specs,
        scratch_shapes=[pltpu.VMEM(s, d) for s, d in scratch],
        input_output_aliases={i: i for i in range(len(into))},
        compiler_params=pltpu.CompilerParams(vmem_limit_bytes=held + extra),
        cost_estimate=cost(us * count, 0),
    )(*skipped, *scalars, *shared, *per_head)


def pair_mask(ids, query_block, blocks, flag, width):
    half = blocks // 2
    lane_block = lanes_of((1, width)) // BLK
    mask = jnp.zeros((1, width), F32)
    for at, key_block in enumerate(ids):
        same = (key_block >= half) == (query_block >= half)
        keep = jnp.where((flag == 1) | same, 1.0, 0.0).astype(F32)
        mask = jnp.where(lane_block == at, keep, mask)
    return mask


def picked(ref, offs):
    return jnp.concatenate([ref[0, pl.ds(o, BLK), :] for o in offs], axis=0)


def listed_blocks(lists_ref, meta_ref, head, block, per_chunk):
    micro, turn = meta_ref[0], meta_ref[1] * per_chunk
    place = block ^ turn
    return [lists_ref[micro, head, place, j] ^ turn for j in range(lists_ref.shape[3])]


def attend_forward_body(
    layer, first_head, meta_ref, lists_ref, n02, n13, f_ref, map_ref, own_ref, *refs
):
    theirs_ref, refs = (refs[0], refs[1:]) if layer == 0 else (None, refs)
    prior, refs = (refs[:2], refs[2:]) if first_head else ((), refs)
    qk_ref, kq_ref, va_ref, pq_ref, pk_ref, sv_ref, corr_ref, es_ref, o_ref = refs[:9]
    a02, a13, qm_scr, nd_scr = refs[9:]
    for old, new in zip(prior, (a02, a13)):
        new[:first_head] = old[...]
    head = first_head + pl.program_id(0)
    flag = meta_ref[2]
    rows = n02.shape[1]
    length = 4 * rows
    blocks = length // BLK
    listed = lists_ref.shape[3]
    feats = f_ref.shape[1]
    lane = lanes_of((rows, LANES))
    low_half = lane < HD
    shift = 0.5 * math.log2(feats)
    proj_scale = HD ** (-0.25) * LOG2E
    norm_scale = 0.5 * HD ** (-0.5) * LOG2E
    own_layer = meta_ref[0] == layer
    fmap = jnp.where(own_layer, f_ref[...], map_ref[3 * HD : 4 * HD, :feats])
    zeros, ones = jnp.zeros_like(fmap), jnp.ones_like(fmap)
    fq = jnp.concatenate([fmap, zeros, ones, zeros], axis=0)
    fk = jnp.concatenate([zeros, fmap, zeros, ones], axis=0)
    weight = []
    for j in range(3):
        place = pl.ds(pl.multiple_of(head * HD, HD), HD)
        if layer == 0:
            theirs = theirs_ref[j * HD : (j + 1) * HD, :]
            weight.append(jnp.where(own_layer, own_ref[j, place, :], theirs))
        else:
            weight.append(own_ref[head, j * HD : (j + 1) * HD, :])
    weight = jnp.concatenate(weight + [jnp.zeros_like(weight[0])], axis=0)
    sums = []
    for at in range(4):
        span = pl.ds(at * rows, rows)
        n = (n13 if at % 2 else n02)[at // 2]
        packed = nt(n, weight).astype(BF).astype(F32)
        qk = packed[:, :LANES]
        va = jnp.where((lane == HD) | (lane == HD + 1), 1.0, packed[:, LANES:]).astype(BF)
        qk_low = qk.astype(BF)
        qk_ref[0, span, :] = qk_low
        kq_ref[0, span, :] = flip(qk).astype(BF)
        qm_scr[span, :] = jnp.where(low_half, qk, 0.0).astype(BF)
        va_ref[0, span, :] = va
        squares = (qk * qk * (-norm_scale / proj_scale)).astype(BF)
        both = jnp.concatenate([qk_low, squares], axis=1)
        phi_q = jnp.exp2(nn(both, fq) * proj_scale - shift)
        pq_ref[0, span, :] = phi_q.astype(BF)
        phi_k = jnp.exp2(nn(both, fk) * proj_scale - shift)
        phi_k = phi_k.astype(BF)
        pk_ref[0, span, :] = phi_k
        sums.append(tn(va, phi_k))
    first = sums[0] + sums[1]
    second = sums[2] + sums[3]
    is_long = flag == 1
    sv_ref[0, 0] = jnp.where(is_long, first + second, first).astype(BF)
    sv_ref[0, 1] = jnp.where(is_long, first + second, second).astype(BF)
    for at in range(4):
        span = pl.ds(at * rows, rows)
        nd_scr[span, :] = nt(pq_ref[0, span, :], sv_ref[0, at // 2])
    score_scale = HD ** (-0.5) * LOG2E
    group = 8

    def step(g):
        todo = []
        for u in range(group):
            qb = g * group + u
            span = pl.ds(qb * BLK, BLK)
            ids = listed_blocks(lists_ref, meta_ref, head, qb, rows // BLK)
            offs = [pl.multiple_of(i * BLK, BLK) for i in ids]
            scores = nt(qm_scr[span, :], picked(kq_ref, offs))
            estimate = nt(pq_ref[0, span, :], picked(pk_ref, offs))
            todo.append((span, ids, offs, qb, scores, estimate))
        ready = []
        for span, ids, offs, qb, scores, estimate in todo:
            mask = pair_mask(ids, qb, blocks, flag, listed * BLK)
            grown = jnp.exp2(scores * score_scale)
            corr = ((grown - estimate) * mask).astype(BF)
            es_ref[0, span, :] = (grown * mask).astype(BF)
            corr_ref[0, span, :] = corr
            ready.append((span, offs, corr))
        for span, offs, corr in ready:
            nd_scr[span, :] += nn(corr, picked(va_ref, offs))

    for g in range(blocks // group):
        step(g)
    half = rows // 2
    for at in range(4):
        span = pl.ds(at * rows, rows)
        nd = nd_scr[span, :]
        inverse = 1.0 / nd[:, HD : HD + 1]
        out = jnp.where(low_half, nd * inverse, inverse)
        o_ref[0, span, :] = out
        pack = jnp.where(low_half[:half], out[:half], flip(out[half:])).astype(BF)
        (a13 if at % 2 else a02)[head, at // 2] = pack


def attend_forward(
    layer, heads, meta, lists, n02, n13, fmap, their_map, weights, prior=(), into=(), deps=()
):
    rows = n02.shape[1]
    length = 4 * rows
    feats = fmap.shape[1]
    pairs = lists.shape[3] * BLK
    outs = [((length, LANES), BF, "hbm")] * 3
    outs += [((length, feats), BF, "hbm")] * 2
    outs += [((2, LANES, feats), BF, "hbm")]
    outs += [((length, pairs), BF, "hbm")] * 2
    outs += [((length, LANES), F32, "hbm")]
    outs += [((heads[1], 2, rows // 2, LANES), BF, "whole")] * 2
    return run_heads(
        functools.partial(attend_forward_body, layer, heads[0]),
        "attend_forward",
        heads,
        outs,
        (meta, lists),
        (n02, n13, fmap, their_map, *weights, *prior),
        (),
        [((length, LANES), BF), ((length, LANES), F32)],
        us=6.0,
        deps=deps,
        into=into,
    )


def attend_backward_body(
    layer, first_head, meta_ref, lists_ref, d02, d13, f_ref, theirs_ref,
    qk_ref, kq_ref, va_ref, pq_ref, pk_ref, sv_ref, corr_ref, es_ref, o_ref, wo_ref,
    out_ref, dna_scr, gt_scr, dpq_scr, dpk_scr, dv_scr, dq_scr, dk_scr,
):
    head = first_head + pl.program_id(0)
    flag = meta_ref[2]
    rows = d02.shape[1]
    length = 4 * rows
    blocks = length // BLK
    listed = lists_ref.shape[3]
    lane = lanes_of((rows, LANES))
    low_half = lane < HD
    weight = wo_ref[0]
    weight = jnp.concatenate([weight, jnp.zeros_like(weight)], axis=0)
    for at in range(4):
        span = pl.ds(at * rows, rows)
        grad = nt((d13 if at % 2 else d02)[at // 2], weight).astype(BF).astype(F32)
        out = o_ref[0, span, :]
        inverse = out[:, HD : HD + 1]
        dd = -jnp.sum(grad * out, axis=1, keepdims=True) * inverse
        dd_high = dd.astype(BF).astype(F32)
        dna = jnp.where(lane == HD, dd_high, grad * inverse)
        dna = jnp.where(lane == HD + 1, dd - dd_high, dna)
        dna_scr[span, :] = dna.astype(BF)
    sums = []
    for at in range(4):
        span = pl.ds(at * rows, rows)
        sums.append(tn(dna_scr[span, :], pq_ref[0, span, :]))
    first = sums[0] + sums[1]
    second = sums[2] + sums[3]
    is_long = flag == 1
    gt_scr[0] = jnp.where(is_long, first + second, first).astype(BF)
    gt_scr[1] = jnp.where(is_long, first + second, second).astype(BF)
    for at in range(4):
        span = pl.ds(at * rows, rows)
        dpq_scr[span, :] = nn(dna_scr[span, :], sv_ref[0, at // 2])
        dpk_scr[span, :] = nn(va_ref[0, span, :], gt_scr[at // 2])
        dv_scr[span, :] = nt(pk_ref[0, span, :], gt_scr[at // 2])
    dk_scr[...] = jnp.zeros_like(dk_scr)
    group = 8

    def step(g):
        todo = []
        for u in range(group):
            qb = g * group + u
            span = pl.ds(qb * BLK, BLK)
            ids = listed_blocks(lists_ref, meta_ref, head, qb, rows // BLK)
            offs = [pl.multiple_of(i * BLK, BLK) for i in ids]
            dc = nt(dna_scr[span, :], picked(va_ref, offs))
            todo.append((span, ids, offs, qb, dc))
        ready = []
        for span, ids, offs, qb, dc in todo:
            mask = pair_mask(ids, qb, blocks, flag, listed * BLK)
            less = (dc * (-mask)).astype(BF)
            ds = (dc * es_ref[0, span, :].astype(F32)).astype(BF)
            ready.append((span, offs, less, ds))
        for span, offs, less, ds in ready:
            dpq_scr[span, :] += nn(less, picked(pk_ref, offs))
            dq_scr[span, :] = nn(ds, picked(kq_ref, offs))
        for span, offs, less, ds in ready:
            to_pk = tn(less, pq_ref[0, span, :])
            to_v = tn(corr_ref[0, span, :], dna_scr[span, :])
            to_k = tn(ds, qk_ref[0, span, :])
            for j, o in enumerate(offs):
                part = slice(j * BLK, (j + 1) * BLK)
                dpk_scr[pl.ds(o, BLK), :] += to_pk[part]
                dv_scr[pl.ds(o, BLK), :] += to_v[part]
                dk_scr[pl.ds(o, BLK), :] += to_k[part]

    for g in range(blocks // group):
        step(g)
    fmap = jnp.where(meta_ref[0] == layer, f_ref[...], theirs_ref[3 * HD : 4 * HD, : f_ref.shape[1]])
    zeros, ones = jnp.zeros_like(fmap), jnp.ones_like(fmap)
    fwide = jnp.concatenate([fmap, zeros, ones, zeros], axis=0)
    for at in range(4):
        span = pl.ds(at * rows, rows)
        both = []
        for d_scr, p_ref, u_ref, direct in (
            (dpq_scr, pq_ref, qk_ref, dq_scr),
            (dpk_scr, pk_ref, kq_ref, dk_scr),
        ):
            t = d_scr[span, :] * p_ref[0, span, :].astype(F32)
            through = nt(t.astype(BF), fwide)
            total = through[:, LANES:]
            near = direct[span, :] - total * u_ref[0, span, :].astype(F32)
            through = through[:, :LANES] * HD ** (-0.25)
            both.append(jnp.where(low_half, through + near * HD ** (-0.5), 0.0))
        out_ref[0, span, :LANES] = (both[0] + flip(both[1])).astype(BF)
        out_ref[0, span, LANES:] = jnp.where(low_half, dv_scr[span, :], 0.0).astype(BF)


def attend_backward(layer, heads, meta, lists, d02, d13, kept, weights, fmap, theirs, deps=()):
    length = kept[0].shape[1]
    feats = fmap.shape[1]
    kept = [pltpu.with_memory_space_constraint(x, pltpu.HBM) for x in kept]
    return run_heads(
        functools.partial(attend_backward_body, layer, heads[0]),
        "attend_backward",
        heads,
        [((length, 2 * LANES), BF, "")],
        (meta, lists),
        (d02, d13, fmap, theirs),
        (*kept, weights),
        [
            ((length, LANES), BF),
            ((2, LANES, feats), BF),
            ((length, feats), F32),
            ((length, feats), F32),
            ((length, LANES), F32),
            ((length, LANES), F32),
            ((length, LANES), F32),
        ],
        us=7.0,
        deps=deps,
    )[0]


def normalize(x, gain, bias):
    center = x - jnp.mean(x, axis=-1, keepdims=True)
    spread = jnp.mean(center * center, axis=-1, keepdims=True)
    return center * lax.rsqrt(spread + EPS) * gain + bias


def normalize_hat(x):
    center = x - jnp.mean(x, axis=-1, keepdims=True)
    spread = jnp.mean(center * center, axis=-1, keepdims=True)
    scale = lax.rsqrt(spread + EPS)
    return center * scale, scale


def normalize_back(hat, scale, gain, grad):
    inner = grad * gain
    mean_one = jnp.mean(inner, axis=-1, keepdims=True)
    mean_two = jnp.mean(inner * hat, axis=-1, keepdims=True)
    return scale * (inner - mean_one - hat * mean_two)


def summed(own_ref, far_ref, at):
    return own_ref[at].astype(F32) + far_ref[1 - at].astype(F32)


def first_rows_body(meta_ref, x0, x2, own_ref, payload_ref, x02, n02, zero_ref, one_ref):
    parts = payload_ref[4 * HD :, :].astype(F32)
    theirs = parts[0:4] + parts[4:8] + parts[8:12]
    own = own_ref[...]
    first = meta_ref[0] == 0
    zero = jnp.where(first, own, theirs)
    zero_ref[...] = zero
    one_ref[...] = jnp.where(first, theirs, own)
    for at, x_ref in enumerate((x0, x2)):
        x = x_ref[...]
        x02[at] = x
        n02[at] = normalize(x.astype(F32), zero[0:1], zero[1:2]).astype(BF)


def first_rows(meta, x0, x2, norms, payload, deps):
    shape = (2,) + x0.shape
    return run_kernel(
        first_rows_body,
        "first_rows",
        [(shape, BF), (shape, BF), (norms.shape, F32), (norms.shape, F32)],
        (meta,),
        (x0, x2, norms, payload),
        deps=deps,
        extra=6 * MIB,
    )


def next_rows_body(mid_ref, own_ref, far_ref, norms_ref, act_ref, x02, n02):
    for at in range(2):
        x = (mid_ref[at] + summed(own_ref, far_ref, at)).astype(BF)
        x02[at] = x
        if at == 0:
            act_ref[...] = x
        n = normalize(x.astype(F32), norms_ref[0:1, :], norms_ref[1:2, :])
        n02[at] = n.astype(BF)


def next_rows(mid, own, far, norms, deps):
    shape = mid.shape
    return run_kernel(
        next_rows_body,
        "next_rows",
        [(shape[1:], BF), (shape, BF), (shape, BF)],
        (),
        (mid, own, far, norms),
        deps=deps,
        extra=6 * MIB,
    )


def last_rows_body(mid_ref, own_ref, far_ref, act_ref):
    act = mid_ref[0] + own_ref[...].astype(F32) + far_ref[...].astype(F32)
    act_ref[...] = act.astype(BF)


def last_rows(mid, own, far, deps):
    return run_kernel(
        last_rows_body, "last_rows", [(own.shape, BF)], (), (mid, own, far), deps=deps
    )[0]


def project_body(p0, p1, p2, p3, s0, s1, s2, s3, x_ref, norms_ref, mid_ref, mixed_ref):
    half = x_ref.shape[1] // 2
    low_half = lanes_of((half, LANES)) < HD
    for slot in range(2):
        total = x_ref[slot].astype(F32)
        for at, (pack, weight) in enumerate(((p0, s0), (p1, s1), (p2, s2), (p3, s3))):
            place = slot if at < 2 else 1 - slot
            left = heads_side_by_side([pack[h, place] for h in range(pack.shape[0])], low_half)
            weight = weight[...]
            spare = left.shape[1] - weight.shape[0]
            if spare:
                weight = jnp.concatenate([weight, jnp.zeros_like(weight[:spare])], axis=0)
            total = total + nn(left, weight)
        mid_ref[slot] = total
        mixed_ref[slot] = normalize(total, norms_ref[2:3, :], norms_ref[3:4, :]).astype(BF)


def project(packs, weights, x02, norms, deps):
    return run_kernel(
        project_body,
        "project",
        [(x02.shape, F32), (x02.shape, BF)],
        (),
        (*packs, *weights, x02, norms),
        us=1.5,
        deps=deps,
        extra=6 * MIB,
    )


def project_back_body(own_ref, far_ref, d_ref, mid_ref, norms_ref, dmid_ref, dproj_ref, dn_ref):
    for at in range(2):
        grad = summed(own_ref, far_ref, at)
        hat, scale = normalize_hat(mid_ref[at])
        dmid = normalize_back(hat, scale, norms_ref[2:3, :], grad) + d_ref[at].astype(F32)
        dmid_ref[at] = dmid
        dproj_ref[at] = dmid.astype(BF)
        if at == 0:
            dn_ref[0:1, :] = jnp.sum(grad * hat, axis=0, keepdims=True)
            dn_ref[1:2, :] = jnp.sum(grad, axis=0, keepdims=True)


def project_back(own, far, d02, mid, norms, deps):
    return run_kernel(
        project_back_body,
        "project_back",
        [(mid.shape, F32), (mid.shape, BF), ((2, mid.shape[2]), F32)],
        (),
        (own, far, d02, mid, norms),
        deps=deps,
        extra=6 * MIB,
    )


def input_back_body(own_ref, far_ref, x_ref, dmid_ref, norms_ref, out_ref, low_ref):
    for at in range(2):
        hat, scale = normalize_hat(x_ref[at].astype(F32))
        grad = summed(own_ref, far_ref, at)
        out = normalize_back(hat, scale, norms_ref[0:1, :], grad) + dmid_ref[at]
        if at == 0:
            out_ref[...] = out
        low_ref[at] = out.astype(BF)


def input_back(own, far, x02, dmid, norms, deps):
    shape = x02.shape
    return run_kernel(
        input_back_body,
        "input_back",
        [(shape[1:], F32), (shape, BF)],
        (),
        (own, far, x02, dmid, norms),
        deps=deps,
        extra=6 * MIB,
    )


def input_last_body(own_ref, far_ref, x_ref, dmid_ref, norms_ref, out_ref, low_ref):
    hat, scale = normalize_hat(x_ref[0].astype(F32))
    grad = own_ref[...].astype(F32) + far_ref[...].astype(F32)
    out = normalize_back(hat, scale, norms_ref[0:1, :], grad) + dmid_ref[0]
    out_ref[...] = out
    low_ref[...] = out.astype(BF)


def input_last(own, far, x02, dmid, norms, deps):
    shape = own.shape
    return run_kernel(
        input_last_body,
        "input_last",
        [(shape, F32), (shape, BF)],
        (),
        (own, far, x02, dmid, norms),
        deps=deps,
        extra=6 * MIB,
    )


def norm_grad_body(stacked, *refs):
    s_refs, x_ref, dn_ref = refs[:-2], refs[-2], refs[-1]
    gain = jnp.zeros((1, dn_ref.shape[1]), F32)
    bias = jnp.zeros((1, dn_ref.shape[1]), F32)
    for at in range(2):
        grad = (s_refs[0][at] if stacked else s_refs[at][...]).astype(F32)
        hat, _ = normalize_hat(x_ref[at].astype(F32))
        gain = gain + jnp.sum(grad * hat, axis=0, keepdims=True)
        bias = bias + jnp.sum(grad, axis=0, keepdims=True)
    dn_ref[0:1, :] = gain
    dn_ref[1:2, :] = bias


def norm_grad(sums, x02, deps):
    return run_kernel(
        functools.partial(norm_grad_body, len(sums) == 1),
        "norm_grad",
        [((2, x02.shape[2]), F32)],
        (),
        (*sums, x02),
        deps=deps,
        extra=6 * MIB,
    )[0]


def gelu_both(hidden):
    cdf = 0.5 * (1.0 + lax.erf(hidden * (0.5**0.5)))
    density = jnp.exp2(hidden * hidden * (-0.5 * LOG2E)) * (2.0 * math.pi) ** (-0.5)
    return hidden * cdf, cdf + hidden * density


def plus_near(value, near, at):
    if near:
        value = value + near[0][at].astype(F32)
    return value.astype(BF)


def plus_pair_body(a_ref, b_ref, out_ref):
    for at in range(2):
        total = a_ref[at].astype(F32) + b_ref[at].astype(F32)
        out_ref[at] = total.astype(BF)


def plus_pair(a, b, deps):
    return run_kernel(plus_pair_body, "plus_pair", [(a.shape, BF)], (), (a, b), deps=deps)[0]


def feed_body(m_ref, up_ref, down_ref, *refs):
    act_ref, slope_ref, p_ref = refs[-3:]
    for at in range(2):
        act, slope = gelu_both(nn(m_ref[at], up_ref[...]))
        act = act.astype(BF)
        act_ref[at] = act
        slope_ref[at] = slope.astype(BF)
        p_ref[at] = plus_near(nn(act, down_ref[...]), refs[:-3], at)


def feed(m, up, down, *near, deps=()):
    hidden = m.shape[:2] + (up.shape[1],)
    return run_kernel(
        feed_body,
        "feed",
        [(hidden, BF), (hidden, BF), (m.shape, BF)],
        (),
        (m, up, down, *near),
        us=1.7,
        deps=deps,
        extra=6 * MIB,
    )


def feed_back_body(d_ref, slope_ref, up_ref, down_ref, *refs):
    dup_ref, p_ref = refs[-2:]
    for at in range(2):
        dup = (nt(d_ref[at], down_ref[...]) * slope_ref[at].astype(F32)).astype(BF)
        dup_ref[at] = dup
        p_ref[at] = plus_near(nt(dup, up_ref[...]), refs[:-2], at)


def feed_back(d, slope, up, down, *near, deps=()):
    return run_kernel(
        feed_back_body,
        "feed_back",
        [(slope.shape, BF), (d.shape, BF)],
        (),
        (d, slope, up, down, *near),
        us=1.7,
        deps=deps,
        extra=6 * MIB,
    )


def feed_turn_body(m_ref, d_ref, up_ref, down_ref, *refs):
    act_ref, dup_ref, p_ref = refs[-3:]
    for at in range(2):
        act, slope = gelu_both(nn(m_ref[at], up_ref[...]))
        act_ref[at] = act.astype(BF)
        dup = (nt(d_ref[at], down_ref[...]) * slope).astype(BF)
        dup_ref[at] = dup
        p_ref[at] = plus_near(nt(dup, up_ref[...]), refs[:-3], at)


def feed_turn(m, d, up, down, *near, deps=()):
    hidden = m.shape[:2] + (up.shape[1],)
    return run_kernel(
        feed_turn_body,
        "feed_turn",
        [(hidden, BF), (hidden, BF), (m.shape, BF)],
        (),
        (m, d, up, down, *near),
        us=2.4,
        deps=deps,
        extra=6 * MIB,
    )


def down_late_body(stacked, act_ref, down_ref, *refs):
    near, outs = (refs[:-1], refs[-1:]) if stacked else (refs[:-2], refs[-2:])
    for at in range(2):
        value = plus_near(nn(act_ref[at], down_ref[...]), near, at)
        if stacked:
            outs[0][at] = value
        else:
            outs[at][...] = value


def down_late(stacked, act, down, *near, deps=()):
    shape = act.shape[:2] + (down.shape[1],)
    return run_kernel(
        functools.partial(down_late_body, stacked),
        "down_late",
        [(shape, BF)] if stacked else [(shape[1:], BF)] * 2,
        (),
        (act, down, *near),
        deps=deps,
    )


def normed_back_body(groups, slots, stacked, *refs):
    lefts = refs[: len(groups)]
    weights = refs[len(groups)]
    rest = refs[len(groups) + 1 :]
    near, outs = (rest[:-1], rest[-1:]) if stacked else (rest[:-2], rest[-2:])
    rows = lefts[0].shape[1] // 4
    for at, slot in enumerate(slots):
        span = pl.ds(slot * rows, rows)
        total, head = None, 0
        for left, count in zip(lefts, groups):
            for h in range(count):
                weight = weights[head]
                part = nn(left[h, span, :][:, : weight.shape[0]], weight)
                total = part if total is None else total + part
                head += 1
        value = plus_near(total, near, at)
        if stacked:
            outs[0][at] = value
        else:
            outs[at][...] = value


def normed_back(slots, stacked, dqkv, weights, *near, deps=()):
    rows = dqkv[0].shape[1] // 4
    width = weights.shape[2]
    groups = tuple(d.shape[0] for d in dqkv)
    return run_kernel(
        functools.partial(normed_back_body, groups, slots, stacked),
        "normed_back",
        [((2, rows, width), BF)] if stacked else [((rows, width), BF)] * 2,
        (),
        (*dqkv, weights, *near),
        us=1.4,
        deps=deps,
        extra=6 * MIB,
    )


def for_section(meta_ref, make, keep, send):
    first = meta_ref[0] == 0

    @pl.when(first)
    def _():
        make(keep, send)

    @pl.when(jnp.logical_not(first))
    def _():
        make(send, keep)


def summed_tn(pairs, left_at, right_at):
    total = None
    for left, right in pairs:
        for at in range(2):
            part = tn(left_at(left, at), right_at(right, at))
            total = part if total is None else total + part
    return total


def feed_grad_body(meta_ref, mix02, mix13, dup02, dup13, act02, act13, d02, d13, keep, send):
    size = keep.shape[0]
    tile = 256 if size % 256 == 0 else size

    def make(first, second):
        ups = ((mix02, dup02), (mix13, dup13))
        downs = ((act02, d02), (act13, d13))
        for out, pairs in ((first, ups), (second, downs)):
            for top in range(0, size, tile):
                total = summed_tn(
                    pairs, lambda x, at: x[at, :, pl.ds(top, tile)], lambda x, at: x[at]
                )
                out[pl.ds(top, tile), :] = total.astype(BF)

    for_section(meta_ref, make, keep, send)


def feed_grad(meta, arrays, deps):
    width, hidden = arrays[0].shape[2], arrays[2].shape[2]
    return run_kernel(
        feed_grad_body,
        "feed_grad",
        [((width, hidden), BF)] * 2,
        (meta,),
        arrays,
        us=2.8,
        deps=deps,
    )


def half_grad_body(meta_ref, left02, left13, right02, right13, keep, send):
    half = keep.shape[0]
    tile = 3 * LANES if half % (3 * LANES) == 0 else half
    for out, which in ((send, 1 - meta_ref[0]), (keep, meta_ref[0])):
        for top in range(0, half, tile):
            span = pl.ds(pl.multiple_of(which * half + top, tile), tile)
            total = summed_tn(
                ((left02, right02), (left13, right13)),
                lambda x, at: x[at, :, span],
                lambda x, at: x[at],
            )
            out[pl.ds(top, tile), :] = total.astype(BF)


def half_grad(meta, left02, left13, right02, right13, deps):
    return run_kernel(
        half_grad_body,
        "half_grad",
        [((left02.shape[2] // 2, right02.shape[2]), BF)] * 2,
        (meta,),
        (left02, left13, right02, right13),
        us=1.4,
        deps=deps,
    )


def heads_side_by_side(own, low_half):
    own = [x.astype(F32) for x in own]
    if len(own) % 2:
        own.append(jnp.zeros_like(own[0]))
    tops, bottoms = [], []
    for h in range(0, len(own), 2):
        tops.append(jnp.where(low_half, own[h], flip(own[h + 1])))
        bottoms.append(jnp.where(low_half, flip(own[h]), own[h + 1]))
    return jnp.concatenate(
        [jnp.concatenate(tops, axis=1), jnp.concatenate(bottoms, axis=1)], axis=0
    ).astype(BF)


def head_grad(dqkv_ref, h, n02, n13):
    rows = n02.shape[1]
    total = None
    for at in range(4):
        n = (n13 if at % 2 else n02)[at // 2]
        part = tn(dqkv_ref[h, pl.ds(at * rows, rows), :], n)
        total = part if total is None else total + part
    return total[: 3 * HD].astype(BF)


def out_grad_rows(a02, a13, d02, d13):
    low_half = lanes_of((a02.shape[2], LANES)) < HD
    total = None
    for at in range(4):
        pack = a13 if at % 2 else a02
        left = heads_side_by_side([pack[h, at // 2] for h in range(pack.shape[0])], low_half)
        part = tn(left, (d13 if at % 2 else d02)[at // 2])
        total = part if total is None else total + part
    return total[: a02.shape[0] * HD].astype(BF)


def head_rows_body(with_out, where, meta_ref, *refs):
    keep, send = refs[-2:]
    refs = refs[:-2]
    half = 3 * HD // 2

    def make(one, two):
        start, rest = 0, refs
        if with_out:
            rows = out_grad_rows(*refs[:4])
            one[:half, :], two[:half, :] = rows[:half], rows[half:]
            start, rest = half, refs[4:]
        for at, (g, h) in enumerate(where):
            rows = head_grad(rest[2 + g], h, rest[0], rest[1])
            place = slice(start + at * half, start + (at + 1) * half)
            one[place, :], two[place, :] = rows[:half], rows[half:]

    for_section(meta_ref, make, keep, send)


def head_rows(with_out, where, meta, arrays, deps):
    count = (with_out + len(where)) * 3 * HD // 2
    return run_kernel(
        functools.partial(head_rows_body, with_out, where),
        "head_rows",
        [((count, arrays[2 if with_out else 0].shape[-1]), BF)] * 2,
        (meta,),
        arrays,
        us=2.0,
        deps=deps,
    )


def both_heads_body(meta_ref, own_ref, *refs):
    theirs, (zero_ref, one_ref) = refs[:-2], refs[-2:]
    first = meta_ref[0] == 0
    for h, their_ref in enumerate(theirs):
        for j in range(3):
            place = slice(j * HD, (j + 1) * HD)
            own, other = own_ref[j, h * HD : (h + 1) * HD, :], their_ref[place, :]
            zero_ref[h, place, :] = jnp.where(first, own, other)
            one_ref[h, place, :] = jnp.where(first, other, own)


def both_heads(meta, own, theirs, deps):
    shape = (own.shape[1] // HD, 3 * HD, own.shape[2])
    return run_kernel(
        both_heads_body, "both_heads", [(shape, BF)] * 2, (meta,), (own, *theirs), deps=deps
    )


def head_payloads_body(rows_ref, fmap_ref, out_ref, norms_ref, *outs):
    for h, ref in enumerate(outs):
        for j in range(3):
            ref[j * HD : (j + 1) * HD, :] = rows_ref[j, h * HD : (h + 1) * HD, :]
    first, last = outs[0], outs[-1]
    width = first.shape[1]
    first[3 * HD : 4 * HD, :] = jnp.zeros((HD, width), BF)
    first[3 * HD : 4 * HD, : fmap_ref.shape[1]] = fmap_ref[...]
    norms = norms_ref[...]
    high, rest = split_float(norms)
    middle = rest.astype(F32)
    low = norms - high.astype(F32) - middle
    parts = [high.astype(F32), middle, low, jnp.zeros((4, width), F32)]
    first[4 * HD :, :] = jnp.concatenate(parts, axis=0).astype(BF)
    last[3 * HD :, :] = out_ref[...]


def head_payloads(rows, fmap, out, norms, deps):
    heads = rows.shape[1] // HD
    counts = [3 * HD] * heads
    counts[0] += HD + 16
    counts[-1] += out.shape[0]
    return run_kernel(
        head_payloads_body,
        "head_payloads",
        [((count, rows.shape[2]), BF) for count in counts],
        (),
        (rows, fmap, out, norms),
        deps=deps,
    )


def held_body(x_ref, out_ref):
    out_ref[...] = x_ref[...]


def held(x, deps):
    return run_kernel(held_body, "held", [(x.shape, x.dtype)], (), (x,), deps=deps)[0]


def touch_body(*refs):
    refs[-1][...] = jnp.zeros_like(refs[-1])


def touch(x, deps):
    return run_kernel(touch_body, "touch", [((8, LANES), F32)], (), (), deps=(x, *deps))[0]


def parts_of_body(parts, pieces, meta_ref, *refs):
    out_ref = refs[-1]
    place = 0
    for i, (start, size) in enumerate(pieces):
        half = refs[i].shape[0] // parts
        shift = (meta_ref[3] & 1) * half if parts > 1 else 0
        out_ref[place : place + size, :] = refs[i][
            pl.ds(pl.multiple_of(start + shift, 16), size), :
        ]
        place += size


def parts_of(meta, parts, pieces, deps):
    arrays = [x for x, _, _ in pieces]
    rows = sum(size for _, _, size in pieces)
    return run_kernel(
        functools.partial(parts_of_body, parts, [(a, b) for _, a, b in pieces]),
        "parts_of",
        [((rows,) + arrays[0].shape[1:], arrays[0].dtype)],
        (meta,),
        arrays,
        deps=deps,
    )[0]


def both_layers_body(parts, pieces, meta_ref, own_ref, *refs):
    zero_ref, one_ref = refs[-2:]
    half = own_ref.shape[0] // parts
    first = meta_ref[0] == 0
    odd = meta_ref[3] & 1
    for side in range(parts):
        which = (odd if side == 0 else 1 - odd) if parts > 1 else 0
        place = 0
        for i, (start, size) in enumerate(pieces):
            theirs = refs[side * len(pieces) + i][start : start + size, :]
            span = pl.ds(pl.multiple_of(which * half + place, 16), size)
            own = own_ref[span, :]
            zero_ref[span, :] = jnp.where(first, own, theirs)
            one_ref[span, :] = jnp.where(first, theirs, own)
            place += size


def both_layers(meta, own, sides, pieces, deps):
    return run_kernel(
        functools.partial(both_layers_body, len(sides), [(a, b) for _, a, b in pieces]),
        "both_layers",
        [(own.shape, BF)] * 2,
        (meta,),
        (own, *[side[i] for side in sides for i, _, _ in pieces]),
        deps=deps,
    )


def split_float(x):
    high = x.astype(BF)
    return high, (x - high.astype(F32)).astype(BF)


def slot_body(items, inputs, meta_ref, *refs):
    outs = refs[inputs:]

    def high(bit):
        return (meta_ref[3] & bit) // bit

    def put(target, rows):
        if target is not None:
            outs[target[0]][target[1] : target[1] + rows.shape[0], :] = rows

    for how, own, came, join, split, out, target in items:
        own = refs[own]
        rows = own.shape[0]
        if how == "norms":
            total = own[...]
            if came is not None:
                extra = refs[came[0]][came[1] : came[1] + 2 * rows, :].astype(F32)
                total = total + (extra[:rows] + extra[rows:])
            outs[out][...] = total
            if target is not None:
                put(target, jnp.concatenate(split_float(total), axis=0))
            continue
        came_ref, first = refs[came[0]], came[1]
        if how == "join":
            side = high(join)
            outs[out][pl.ds(pl.multiple_of(side * rows, 16), rows), :] = own[...]
            other_side = pl.ds(pl.multiple_of((1 - side) * rows, 16), rows)
            outs[out][other_side, :] = came_ref[first : first + rows, :]
            if target is not None:
                put(target, outs[out][...])
            continue
        if split is None:
            total = own[...].astype(F32) + came_ref[first : first + rows, :].astype(F32)
            outs[out][...] = total.astype(BF)
            put(target, total.astype(BF))
            continue
        half = rows // 2
        side = high(split)
        for which, place in ((side, None), (1 - side, target)):
            mine = pl.ds(pl.multiple_of(which * half, 16), half)
            theirs = pl.ds(pl.multiple_of(first + which * half, 16), half)
            total = (own[mine, :].astype(F32) + came_ref[theirs, :].astype(F32)).astype(BF)
            if place is None:
                outs[out][...] = total
            else:
                put(place, total)


def norm_rows_body(*refs):
    total = jnp.concatenate([r[...] for r in refs[:-2]], axis=0)
    refs[-2][...] = total
    refs[-1][...] = jnp.concatenate(split_float(total), axis=0)


def norm_rows(parts, deps):
    rows, width = sum(x.shape[0] for x in parts), parts[0].shape[1]
    return run_kernel(
        norm_rows_body,
        "norm_rows",
        [((rows, width), F32), ((2 * rows, width), BF)],
        (),
        parts,
        deps=deps,
    )


def finish_rows_body(zero_count, one_count, meta_ref, *refs):
    zeros = refs[:zero_count]
    ones = refs[zero_count : zero_count + one_count]
    got_ref, out_ref, q_ref = refs[zero_count + one_count :]
    half = 3 * HD // 2
    first = meta_ref[0] == 0

    def rows(refs, start):
        for ref in refs:
            if start < ref.shape[0]:
                return ref[start : start + half, :]
            start -= ref.shape[0]

    for piece in range(got_ref.shape[0] // half):
        start = piece * half
        mine = jnp.where(first, rows(zeros, start), rows(ones, start)).astype(F32)
        got = got_ref[start : start + half, :].astype(F32)
        both = [jnp.where(first, mine, got), jnp.where(first, got, mine)]
        both = jnp.concatenate(both, axis=0)
        if piece == 0:
            out_ref[...] = both
        else:
            place = slice((piece - 1) * HD, piece * HD)
            for j in range(3):
                q_ref[j, place, :] = both[j * HD : (j + 1) * HD]


def finish_rows(meta, zeros, ones, got, deps):
    heads = got.shape[0] // (3 * HD // 2) - 1
    width = got.shape[1]
    return run_kernel(
        functools.partial(finish_rows_body, len(zeros), len(ones)),
        "finish_rows",
        [((3 * HD, width), F32), ((3, heads * HD, width), F32)],
        (meta,),
        (*zeros, *ones, got),
        deps=deps,
    )


class Sum:
    def __init__(self, own, came, bits, norms=False):
        self.own, self.came, self.norms = own, came, norms
        self.bits, self.halved, self.at = bits, [], 0
        self.done = False

    def plan(self):
        if self.at <= len(self.bits):
            last = self.at == len(self.bits)
            self.at += 1
            if self.norms:
                return "norms", None, None, None if last else self.bits[self.at - 1]
            if last:
                return "add", None, None, self.halved[-1] if self.halved else None
            bit = self.bits[self.at - 1]
            if self.own.shape[0] % 32 == 0:
                self.halved.append(bit)
                return "add", None, bit, bit
            return "add", None, None, bit
        bit = self.halved.pop()
        return "join", bit, None, self.halved[-1] if self.halved else None


def slot(order, meta, sums):
    sums = [x for x in sums if not x.done]
    if not sums:
        return
    width = sums[0].own.shape[1]
    arrays, outs, items, sent = [], [], [], {}
    plans = [x.plan() for x in sums]

    def index(x):
        for i, a in enumerate(arrays):
            if a is x:
                return i
        arrays.append(x)
        return len(arrays) - 1

    for x, (how, join, split, _) in zip(sums, plans):
        rows = x.own.shape[0]
        if split is not None:
            rows //= 2
        if how == "join":
            rows *= 2
        outs.append(((rows, width), F32 if x.norms else BF))
    bundles = sorted({plan[3] for plan in plans if plan[3] is not None})
    sizes = {bit: 0 for bit in bundles}
    for i, (x, (how, join, split, bit)) in enumerate(zip(sums, plans)):
        target = None
        if bit is not None:
            target = (len(sums) + bundles.index(bit), sizes[bit])
            sent[i] = (bit, sizes[bit])
            sizes[bit] += outs[i][0][0] * (2 if x.norms else 1)
        came = None if x.came is None else (index(x.came[0]), x.came[1])
        items.append((how, index(x.own), came, join, split, i, target))
    outs += [((sizes[bit], width), BF) for bit in bundles]
    results = order.kernel(
        run_kernel,
        functools.partial(slot_body, items, len(arrays)),
        "slot",
        outs,
        (meta,),
        arrays,
    )
    came = {
        bit: order.send(results[len(sums) + i], "dp", bit) for i, bit in enumerate(bundles)
    }
    for i, x in enumerate(sums):
        x.own = results[i]
        x.done = i not in sent
        if not x.done:
            x.came = (came[sent[i][0]], sent[i][1])


def swap(x, axis, bit):
    size = lax.axis_size(axis)
    return lax.ppermute(x, axis, [(i, i ^ bit) for i in range(size)])


def after(x, *others):
    return lax.optimization_barrier((x, *others))[0]


class Order:
    def __init__(self):
        self.last = ()

    def __call__(self, x):
        if self.last:
            x = after(x, *self.last)
        return x

    def done(self, *results):
        self.last = results[:1]
        return results[0] if len(results) == 1 else results

    def kernel(self, fn, *args, **kwargs):
        outs = fn(*args, deps=self.last, **kwargs)
        self.last = (outs[0] if isinstance(outs, (list, tuple)) else outs,)
        return outs

    def plain(self, fn, first, *rest):
        return self.done(fn(self(first), *rest))

    def send(self, x, axis, bit):
        return swap(self.done(self(x)), axis, bit)


def body(
    tokens, w_qkv, w_out, w_up, w_down, norm_params, features, block_lists, long_flags, out_grad
):
    section_id = lax.axis_index("section")
    is_first = section_id == 0
    dp_id = lax.axis_index("dp")
    dp_size = lax.axis_size("dp")
    dp_bits = [1 << i for i in range(dp_size.bit_length() - 1)]
    width = tokens.shape[2]
    heads = w_out.shape[1] // HD
    order = Order()

    def pick(x):
        return lax.dynamic_index_in_dim(x, section_id, 0, keepdims=False)

    def other(x):
        return order.send(x, "section", 1)

    def near(x):
        return order.send(x, "tensor", 1)

    def far(x):
        return order.send(x, "tensor", 2)

    def to_section(x, target):
        return lax.ppermute(order.done(order(x)), "section", [(1 - target, target)])

    def choose_zero(own, theirs):
        return jnp.where(is_first, own, theirs)

    def choose_one(own, theirs):
        return jnp.where(is_first, theirs, own)

    kept = [{}, {}]
    w = [{}, {}]
    meta = [section_id, lax.axis_index("tensor"), pick(long_flags), dp_id]
    meta = jnp.stack(meta).astype(jnp.int32)

    parts = 1 if dp_size % 2 else 2
    own_q = w_qkv[0].transpose(1, 2, 0)
    payloads = order.kernel(head_payloads, own_q, features[0], w_out[0], norm_params[0])
    theirs_q = [other(payloads[0])]
    x_rows = order.plain(pick, tokens)
    x_far = far(x_rows)
    theirs_q += [other(x) for x in payloads[1:]]
    order.kernel(touch, block_lists)
    order.kernel(touch, theirs_q[1])
    x02, n02, w[0]["norms"], w[1]["norms"] = order.kernel(
        first_rows, meta, x_rows, x_far, norm_params[0], theirs_q[0]
    )
    n13 = near(n02)

    sizes = [x.shape[1] // parts for x in (w_up, w_down)]
    third = sum(sizes) // 3
    cuts = [
        [(w_up[0], 0, third)],
        [(w_up[0], third, sizes[0] - third), (w_down[0], 0, 2 * third - sizes[0])],
        [(w_down[0], 2 * third - sizes[0], third)],
    ]
    came = []
    sides = [came] if parts == 1 else [came, []]

    def share(i):
        if parts > 1:
            piece = came[i]
            if i:
                piece = held(piece, deps=(kept[0]["packs"][0],))
            sides[1].append(order.send(piece, "dp", 1))

    def forward_heads(layer, first, end, weights, packs=()):
        k = kept[layer]
        outs = order.kernel(
            attend_forward,
            layer,
            (first, end, heads),
            meta,
            block_lists,
            k["n02"],
            k["n13"],
            features[0],
            theirs_q[0],
            weights,
            packs,
            k["kept"],
        )
        k["kept"] = outs[:9]
        order.done(outs[9])
        return outs[9:]

    def new_layer(layer, x02, n02, n13):
        kept[layer].update(x=x02, n02=n02, n13=n13, kept=())

    def gathered(packs):
        a02, a13 = packs
        return [a02, near(a13), far(a02), order.send(a13, "tensor", 3)]

    new_layer(0, x02, n02, n13)
    k = kept[0]
    packs = ()
    for h in range(heads):
        if h == 2:
            w[0]["out"], w[1]["out"] = order.kernel(
                both_layers, meta, w_out[0], [theirs_q[-1:]], [(0, 3 * HD, w_out.shape[1])]
            )
            out_far = far(w[0]["out"])
            out_near = near(w[0]["out"])
        packs = forward_heads(0, h, h + 1, (own_q, theirs_q[h]), packs)
        if h == 0:
            came += [other(order.kernel(parts_of, meta, parts, cut)) for cut in cuts]
        elif h == 1:
            share(0)
    k["packs"] = packs
    a02, a13 = packs
    packs = [a02, near(a13), far(a02), order.send(a13, "tensor", 3)]
    order.kernel(touch, out_near)
    order.kernel(touch, packs[1])
    order.kernel(touch, sides[-1][0])
    out_last = near(out_far)
    share(1)
    order.kernel(touch, out_last)
    share(2)
    w[0]["shards"] = [w[0]["out"], out_near, out_far, out_last]
    w[0]["up"], w[1]["up"] = order.kernel(
        both_layers, meta, w_up[0], sides, [(0, 0, third), (1, 0, sizes[0] - third)]
    )
    w[0]["down"], w[1]["down"] = order.kernel(
        both_layers,
        meta,
        w_down[0],
        sides,
        [(1, sizes[0] - third, 2 * third - sizes[0]), (2, 0, third)],
    )
    k["mid"], k["mix02"] = order.kernel(project, packs, w[0]["shards"], x02, w[0]["norms"])
    k["mix13"] = near(k["mix02"])
    k["act02"], k["slope02"], sums = order.kernel(feed, k["mix02"], w[0]["up"], w[0]["down"])
    k["act13"], k["slope13"], part = order.kernel(feed, k["mix13"], w[0]["up"], w[0]["down"])
    sums = order.kernel(plus_pair, sums, near(part))
    sums_far = far(sums)
    given = order.plain(pick, out_grad)
    given_far = far(given)
    out_near, out_far = near(w[1]["out"]), far(w[1]["out"])
    w[0]["q"], w[1]["q"] = order.kernel(both_heads, meta, own_q, theirs_q)
    acts_zero, x02, n02 = order.kernel(next_rows, k["mid"], sums, sums_far, w[1]["norms"])
    n13 = near(n02)

    new_layer(1, x02, n02, n13)
    k = kept[1]
    k["packs"] = forward_heads(1, 0, heads, (w[1]["q"],))
    packs = gathered(k["packs"])
    w[1]["shards"] = [w[1]["out"], out_near, out_far, near(out_far)]
    given02 = order.plain(lambda a, b: jnp.stack([a, b]), given, given_far)
    given13 = near(given02)
    k["mid"], k["mix02"] = order.kernel(project, packs, w[1]["shards"], x02, w[1]["norms"])
    k["mix13"] = near(k["mix02"])
    d02, d13 = given02, given13
    k["act02"], dup02, sums = order.kernel(
        feed_turn, k["mix02"], d02, w[1]["up"], w[1]["down"]
    )
    k["act13"], dup13, part = order.kernel(
        feed_turn, k["mix13"], d13, w[1]["up"], w[1]["down"]
    )
    sums = order.kernel(plus_pair, sums, near(part))
    sums_far = far(sums)

    keep, send = order.kernel(half_grad, meta, k["act02"], k["act13"], d02, d13)
    down_one = Sum(keep, (other(send), 0), dp_bits)
    keep, send = order.kernel(half_grad, meta, k["mix02"], k["mix13"], dup02, dup13)
    up_one = Sum(keep, (other(send), 0), dp_bits)
    late_part = near(order.kernel(down_late, True, k["act13"], w[1]["down"])[0])
    dmid, dproj02, norm_two = order.kernel(
        project_back, sums, sums_far, d02, k["mid"], w[1]["norms"]
    )
    dproj13 = near(dproj02)
    slot(order, meta, [down_one])
    late_own, late_send = order.kernel(down_late, False, k["act02"], w[1]["down"], late_part)
    late_far = far(late_send)
    dqkv = order.kernel(
        attend_backward,
        1,
        (0, heads, heads),
        meta,
        block_lists,
        dproj02,
        dproj13,
        k["kept"],
        w[1]["out"].reshape(heads, HD, width),
        features[0],
        theirs_q[0],
    )
    acts_one = order.kernel(last_rows, k["mid"], late_own, late_far)
    slot(order, meta, [down_one, up_one])
    part = near(order.kernel(normed_back, (1, 3), True, [dqkv], w[1]["q"])[0])
    keep, send = order.kernel(
        head_rows,
        True,
        [(0, h) for h in range(heads)],
        meta,
        (*k["packs"], dproj02, dproj13, k["n02"], k["n13"], dqkv),
    )
    rows_one = Sum(keep, (other(send), 0), dp_bits)
    sums = order.kernel(normed_back, (0, 2), True, [dqkv], w[1]["q"], part)[0]
    sums_far = far(sums)
    acts_came = other(order.plain(choose_one, acts_zero, acts_one))
    norm_one = order.kernel(norm_grad, [sums], k["x"])
    norms_one = [norm_one, norm_two]
    slot(order, meta, [down_one, up_one, rows_one])
    grad_one, d02 = order.kernel(input_back, sums, sums_far, k["x"], dmid, w[1]["norms"])

    d13 = near(d02)
    k = kept[0]
    dup02, sums = order.kernel(feed_back, d02, k["slope02"], w[0]["up"], w[0]["down"])
    dup13, part = order.kernel(feed_back, d13, k["slope13"], w[0]["up"], w[0]["down"])
    part = near(part)
    keep, send = order.kernel(half_grad, meta, k["act02"], k["act13"], d02, d13)
    down = Sum(keep, (other(send), 0), dp_bits)
    sums = order.kernel(plus_pair, sums, part)
    order.kernel(touch, acts_came)
    sums_far = far(sums)
    keep, send = order.kernel(half_grad, meta, k["mix02"], k["mix13"], dup02, dup13)
    up = Sum(keep, (other(send), 0), dp_bits)
    slot(order, meta, [down_one, up_one, rows_one, down])
    dmid, dproj02, norm_two = order.kernel(
        project_back, sums, sums_far, d02, k["mid"], w[0]["norms"]
    )
    dproj13 = near(dproj02)
    keep, send = order.kernel(head_rows, True, (), meta, (*k["packs"], dproj02, dproj13))
    out = Sum(keep, (other(send), 0), dp_bits)
    dqkv = order.kernel(
        attend_backward,
        0,
        (0, heads, heads),
        meta,
        block_lists,
        dproj02,
        dproj13,
        k["kept"],
        w[0]["out"].reshape(heads, HD, width),
        features[0],
        theirs_q[0],
    )
    step = functools.partial(slot, order, meta)
    step([down_one, down, up, out])
    order.kernel(touch, up_one.came[0])
    part = near(order.kernel(normed_back, (1, 3), True, [dqkv], w[0]["q"])[0])
    keep, send = order.kernel(
        head_rows, False, [(0, h) for h in range(heads)], meta, (k["n02"], k["n13"], dqkv)
    )
    rows = Sum(keep, (other(send), 0), dp_bits)
    own, send = order.kernel(normed_back, (0, 2), False, [dqkv], w[0]["q"], part)
    send_far = far(send)
    norm_one = order.kernel(norm_grad, [own, send], k["x"])
    norms, send = order.kernel(norm_rows, (norm_one, norm_two, *norms_one))
    norms = Sum(norms, (other(send), 0), dp_bits, norms=True)
    step([up, out])
    step([down])
    step([rows, norms])
    step([rows, norms])
    grad_zero, low_zero = order.kernel(input_last, own, send_far, k["x"], dmid, w[0]["norms"])
    order.kernel(touch, acts_came)
    grads_came = other(order.plain(choose_one, low_zero, d02[0]))
    gots = {}

    def swap_done():
        for name, zero, one in (("down", down, down_one), ("up", up, up_one)):
            if name not in gots and zero.done and one.done:
                gots[name] = other(order.plain(choose_one, zero.own, one.own))

    step([up_one])
    swap_done()
    step([rows_one])
    swap_done()
    step([up, out])
    swap_done()
    step([down])
    swap_done()
    order.kernel(touch, grads_came)
    step([up_one])
    swap_done()
    step([rows_one, up, out])
    swap_done()
    step([down])
    swap_done()
    step([rows, norms])
    swap_done()
    step([up, out])
    swap_done()
    step([rows_one])
    swap_done()
    step([rows, norms])
    swap_done()
    left = [down_one, up_one, rows_one, down, up, out, rows, norms]
    while any(not x.done for x in left):
        step(left)
        swap_done()
    rows_zero = order.plain(lambda a, b: jnp.concatenate([a, b], axis=0), out.own, rows.own)
    rows_got = other(order.plain(choose_one, rows_zero, rows_one.own))
    norms = norms.own
    norms = order.plain(jnp.add, norms, near(norms))
    norms = order.plain(jnp.add, norms, far(norms))

    def choose(a, b):
        return jnp.where(is_first, a, b).astype(F32)

    def both_halves(zero, one, got):
        mine = jnp.where(is_first, zero, one)
        return jnp.concatenate([choose(mine, got), choose(got, mine)], axis=0)

    grad_down = both_halves(down.own, down_one.own, gots["down"])
    grad_up = both_halves(up.own, up_one.own, gots["up"])
    grad_o, grad_q = order.kernel(
        finish_rows, meta, (out.own, rows.own), (rows_one.own,), rows_got
    )
    grad_q = grad_q.transpose(2, 0, 1)
    grad_n = pick(norms.reshape(2, 4, width))

    def by_layer(mine, came):
        came = came.astype(mine.dtype)
        return jnp.stack([jnp.where(is_first, mine, came), jnp.where(is_first, came, mine)])[None]

    acts = by_layer(choose_zero(acts_zero, acts_one), acts_came)
    input_grads = by_layer(choose_zero(grad_zero, grad_one), grads_came)
    return (
        acts,
        input_grads,
        grad_q[None],
        grad_o[None],
        grad_up[None],
        grad_down[None],
        grad_n[None],
    )


def solution(mesh):
    in_specs = (
        P("dp", "tensor", None),
        P("section", None, None, "tensor"),
        P("section", "tensor", None),
        P("section", None, "tensor"),
        P("section", "tensor", None),
        P("section", None, None),
        P("section", None, None),
        P("dp", "tensor", None, None),
        P("dp"),
        P("dp", "tensor", None),
    )
    out_specs = (
        P("section", "dp", "tensor", None),
        P("section", "dp", "tensor", None),
        P("section", None, None, "tensor"),
        P("section", "tensor", None),
        P("section", None, "tensor"),
        P("section", "tensor", None),
        P("section", None, None),
    )
    return jax.shard_map(body, mesh=mesh, in_specs=in_specs, out_specs=out_specs, check_vma=False)
```
